32 devices in a mesh: dp: 8 (over z, core), tensor: 4 (over y, x).
Axes of the slice: x: 2, y: 2, z: 4, core: 2. Of those that a mesh axis runs over, the one named last changes fastest.
Arguments:
- requests: bfloat16 [512, 8192], P('dp'), may hold values from -6 to 6
- base_gate_up_weight: bfloat16 [8192, 2, 28672], P('dp', None, 'tensor'), may hold values from -0.0625 to 0.0625
- adapter_down_weight: bfloat16 [64, 8192, 128], P('dp', 'tensor'), may hold values from -0.0625 to 0.0625
- adapter_up_weight: bfloat16 [64, 64, 2, 28672], P('dp', None, None, 'tensor'), may hold values from -0.75 to 0.75
- request_adapter: int32 [512], P('dp'), may hold values from 0 to 63, as said below
- adapter_position: int32 [64], replicated, may hold values from 0 to 63, as said below
- counts: int32 [8], replicated, may hold values from 1 to 64, 384 in all
Outputs:
- hidden: bfloat16 [512, 28672], P('dp', 'tensor')
The draws below stay inside these ranges and needn't reach their ends.
Inputs may be any that keep to these rules, and one draw needn't show every extreme that they name: `request_adapter`: the owner of store position s is s // 8. Among the 64 rows of one group at most 8 use adapters of one owner; in every draw one owner receives exactly 8 rows from every group. `adapter_position`: each store position appears once. `counts`: rows of a group past its count are padding.
All inputs are finite; a program needn't handle non-finite values.
Results may differ from the reference program's by a relative error of at most 0.0058.
Values may be sent and summed in bfloat16 or wider, within the bound.
No kernel may reach another device: no remote copies, remote signals or barrier semaphores. Data moves between devices by JAX's collectives and lax.ppermute only.
A program may use at most 192 MiB of HBM per device.

```python
import math
import jax
import jax.numpy as jnp
import numpy as np
from jax import lax

MODEL_WIDTH = 8192
HIDDEN_UNITS = 28672
ADAPTER_RANK = 64
R = 64
PER_OWNER = 8
CAP = 8
ROWS = 512
ADAPTER_TOTAL = 64
N_DP = 8


def adapter_table(key):
    return jax.random.permutation(jax.random.fold_in(key, 11), ADAPTER_TOTAL).astype(jnp.int32)


def draw_adapter_position(key, part):
    return adapter_table(key)


def draw_request_adapter(key, part):
    table = adapter_table(key)
    inverse = jnp.zeros((ADAPTER_TOTAL,), jnp.int32).at[table].set(jnp.arange(ADAPTER_TOTAL, dtype=jnp.int32))
    busiest = jax.random.randint(jax.random.fold_in(key, 12), (), 0, N_DP).astype(jnp.int32)
    total_slots = N_DP * CAP

    def one_group(index):
        sub = jax.random.fold_in(jax.random.fold_in(key, 13), index)
        order = jax.random.permutation(jax.random.fold_in(sub, 1), total_slots).astype(jnp.int32)
        owner = order // CAP
        ranking = jnp.where(owner == busiest, 0, 1) * total_slots + jnp.arange(total_slots, dtype=jnp.int32)
        picked = owner[jnp.argsort(ranking)][:R]
        mixed = jax.random.permutation(jax.random.fold_in(sub, 2), picked)
        local = jax.random.randint(jax.random.fold_in(sub, 3), (R,), 0, PER_OWNER).astype(jnp.int32)
        return inverse[mixed * PER_OWNER + local]
    return jax.vmap(one_group)(jnp.arange(N_DP, dtype=jnp.int32)).reshape(ROWS).astype(jnp.int32)


def level_of(key, dims, shards, smallest, top_value):
    loudness = 1.0
    for dim, shards_of in shards:
        steps = jax.random.uniform(jax.random.fold_in(jax.random.fold_in(key, 6), dim), (shards_of,), jnp.float32, smallest / len(shards), top_value / len(shards))
        loudness = loudness * jnp.repeat(jnp.exp(steps), dims[dim] // shards_of).reshape((-1,) + (1,) * (len(dims) - 1 - dim))
    return loudness


def length_profile(amount, total, limit, skew):
    weights = [(1 << 20) // math.isqrt(grade ** skew) + 1 for grade in range(2, amount + 1)]
    rest, holding = total - limit - (amount - 1), [1] * (amount - 1)
    while rest > 0:
        candidates = [i for i in range(amount - 1) if holding[i] < limit]
        mass, budget = sum([weights[i] for i in candidates]), rest
        for i in candidates:
            addition = min(limit - holding[i], max(1, budget * weights[i] // mass), rest)
            holding[i] = holding[i] + addition
            rest = rest - addition
    return np.array([limit] + holding)


def ragged(key, number_of, total, reach, slope):
    if number_of == 2:
        one = jax.random.randint(key, (), max(1, total - reach), min(reach, total - 1) + 1)
        return jnp.stack([one, total - one])
    sizes = jnp.asarray(length_profile(number_of, total, reach, slope), jnp.int32)
    couples = (number_of - 1) // 2
    source_of, sink = sizes[1:1 + 2 * couples:2], sizes[2:2 + 2 * couples:2]
    room = jnp.minimum(source_of - 1, reach - sink)
    passed = jax.random.randint(jax.random.fold_in(key, 1), (couples,), 0, 1 << 20) % (room + 1)
    sizes = sizes.at[1:1 + 2 * couples:2].set(source_of - passed).at[2:2 + 2 * couples:2].set(sink + passed)
    return sizes[jax.random.permutation(jax.random.fold_in(key, 2), number_of)]


def bell_draw(rng, dims, scale, bound, shards=(), kind=jnp.bfloat16):
    result = jax.random.normal(rng, dims, jnp.float32) * scale
    if len(shards) > 0:
        result = level_of(rng, dims, shards, -0.22, 0.18) * result
    return jnp.clip(result, min=-bound, max=bound).astype(kind)


def setup_inputs(seed: int = 0) -> dict:
    arg_keys = jax.random.split(jax.random.key(seed), 8)
    return {
        "requests": bell_draw(arg_keys[0], (ROWS, MODEL_WIDTH), 1.0, 6.0, ((0, 8),)),
        "base_gate_up_weight": bell_draw(arg_keys[1], (MODEL_WIDTH, 2, HIDDEN_UNITS), MODEL_WIDTH ** -0.5, 0.0625, ((0, 8), (2, 4))),
        "adapter_down_weight": bell_draw(arg_keys[2], (ADAPTER_TOTAL, MODEL_WIDTH, 2 * ADAPTER_RANK), MODEL_WIDTH ** -0.5, 0.0625, ((0, 8), (1, 4))),
        "adapter_up_weight": bell_draw(arg_keys[3], (ADAPTER_TOTAL, ADAPTER_RANK, 2, HIDDEN_UNITS), ADAPTER_RANK ** -0.5, 0.75, ((0, 8), (3, 4))),
        "request_adapter": draw_request_adapter(jax.random.fold_in(arg_keys[7], 71), 0),
        "adapter_position": draw_adapter_position(jax.random.fold_in(arg_keys[7], 71), 0),
        "counts": ragged(arg_keys[6], N_DP, 3 * R * N_DP // 4, R, 2).astype(jnp.int32),
    }


def reference(requests, base_gate_up_weight, adapter_down_weight, adapter_up_weight, request_adapter, adapter_position, counts):
    slot = adapter_position[request_adapter].astype(jnp.int32)

    def one_row(pair):
        row, store_location = pair
        down_matrix = lax.dynamic_index_in_dim(adapter_down_weight, store_location, 0, keepdims=False)
        down = jnp.dot(row[None, :], down_matrix, preferred_element_type=jnp.float32).astype(jnp.bfloat16)[0]
        up_matrix = lax.dynamic_index_in_dim(adapter_up_weight, store_location, 0, keepdims=False)
        term_gate = jnp.dot(down[None, :ADAPTER_RANK], up_matrix[:, 0, :], preferred_element_type=jnp.float32)[0]
        term_up = jnp.dot(down[None, ADAPTER_RANK:], up_matrix[:, 1, :], preferred_element_type=jnp.float32)[0]
        return jnp.stack([term_gate, term_up]).astype(jnp.bfloat16)

    delta = lax.map(one_row, (requests, slot), batch_size=16)
    gate = jnp.dot(requests, base_gate_up_weight[:, 0, :], preferred_element_type=jnp.float32) + delta[:, 0, :].astype(jnp.float32)
    up = jnp.dot(requests, base_gate_up_weight[:, 1, :], preferred_element_type=jnp.float32) + delta[:, 1, :].astype(jnp.float32)
    position = jnp.arange(ROWS, dtype=jnp.int32)
    live = (position % R) < counts[position // R]
    hidden = jnp.where(live[:, None], jax.nn.silu(gate) * up, 0.0)
    return hidden.astype(jnp.bfloat16)
```

```python
import functools

import jax
import jax.numpy as jnp
from jax import lax
from jax.experimental import pallas as pl
from jax.experimental.pallas import tpu as pltpu
from jax.sharding import PartitionSpec as P

CHUNKS = 7


def partial_kernel(x_ref, d_ref, w_ref, u_ref, own_ref, other_ref):
    half = own_ref.shape[1]
    for t in range(2):
        total = jnp.dot(x_ref[...], w_ref[t], preferred_element_type=jnp.float32)
        total = total + jnp.dot(d_ref[t], u_ref[t], preferred_element_type=jnp.float32)
        own_ref[t] = total[:half]
        other_ref[t] = total[half:].astype(jnp.bfloat16)


def partial_sums(x, d, w, u, chunk, width, block):
    rows, depth = x.shape
    inner = d.shape[2]
    per = width // block
    return pl.pallas_call(
        partial_kernel,
        grid=(per,),
        in_specs=[
            pl.BlockSpec((rows, depth), lambda j: (0, 0)),
            pl.BlockSpec((2, rows, inner), lambda j: (0, 0, 0)),
            pl.BlockSpec((2, depth, block), lambda j: (0, 0, chunk * per + j)),
            pl.BlockSpec((2, inner, block), lambda j: (0, 0, chunk * per + j)),
        ],
        out_specs=[
            pl.BlockSpec((2, rows // 2, block), lambda j: (0, 0, j)),
            pl.BlockSpec((2, rows // 2, block), lambda j: (0, 0, j)),
        ],
        out_shape=[
            jax.ShapeDtypeStruct((2, rows // 2, width), jnp.float32),
            jax.ShapeDtypeStruct((2, rows // 2, width), jnp.bfloat16),
        ],
        compiler_params=pltpu.CompilerParams(vmem_limit_bytes=40 * 2**20),
        cost_estimate=pl.CostEstimate(
            flops=4 * rows * (depth + inner) * width,
            bytes_accessed=4 * (depth + inner) * width + 6 * rows * width,
            transcendentals=0,
        ),
    )(x, d, w, u)


def reversed_bits(value, bits):
    out = 0
    for _ in range(bits):
        out = out * 2 + value % 2
        value //= 2
    return out


def body(
    requests,
    base_gate_up_weight,
    adapter_down_weight,
    adapter_up_weight,
    request_adapter,
    adapter_position,
    counts,
):
    rows, width = requests.shape
    groups = lax.axis_size("dp")
    lanes = lax.axis_size("tensor")
    holder_adapters, depth_part, rank_doubled = adapter_down_weight.shape
    rank = rank_doubled // 2
    extent = adapter_up_weight.shape[3]
    capacity = rows // 8
    buffer = groups * capacity
    group = lax.axis_index("dp")
    lane = lax.axis_index("tensor")
    bits = groups.bit_length() - 1
    f32, bf16, i32 = jnp.float32, jnp.bfloat16, jnp.int32

    match = request_adapter[:, None] == jnp.arange(adapter_position.shape[0], dtype=i32)[None, :]
    slot = jnp.sum(jnp.where(match, adapter_position[None, :], 0), axis=1)
    owner = slot // holder_adapters
    local = slot % holder_adapters
    owner_hot = (owner[:, None] == jnp.arange(groups, dtype=i32)[None, :]).astype(i32)
    place = jnp.sum(owner_hot * (jnp.cumsum(owner_hot, axis=0) - 1), axis=1)
    target = owner * capacity + place
    select = (target[None, :] == jnp.arange(buffer, dtype=i32)[:, None]).astype(bf16)
    row_index = jnp.arange(rows, dtype=i32)
    piece = lax.dynamic_slice_in_dim(requests, lane * depth_part, depth_part, 1)
    column = jnp.arange(128, dtype=i32)[None, :]
    labels = jnp.where(column == 0, local[:, None], jnp.where(column == 1, row_index[:, None], 0))
    outgoing = jnp.dot(
        select, jnp.concatenate([piece, labels.astype(bf16)], axis=1), preferred_element_type=f32
    ).astype(bf16)
    arrived = lax.all_to_all(outgoing, "dp", split_axis=0, concat_axis=0, tiled=True)
    spread = lax.all_to_all(requests, "dp", split_axis=1, concat_axis=0, tiled=True)

    gate_up = base_gate_up_weight.transpose(1, 0, 2)
    adapter_up = adapter_up_weight.reshape(holder_adapters * rank, 2, extent).transpose(1, 0, 2)

    which = arrived[:, depth_part].astype(i32)
    place_row = arrived[:, depth_part + 1].astype(i32)
    mine = which[:, None] == jnp.arange(holder_adapters, dtype=i32)[None, :]
    routed = arrived[:, :depth_part]
    spaced = jnp.where(mine[:, :, None], routed[:, None, :], jnp.zeros((), bf16))
    part_down = jnp.dot(
        spaced.reshape(buffer, holder_adapters * depth_part),
        adapter_down_weight.reshape(holder_adapters * depth_part, rank_doubled),
        preferred_element_type=f32,
    )
    total_down = part_down
    for step in range(1, lanes):
        total_down = total_down + lax.ppermute(
            part_down, "tensor", [(i, i ^ step) for i in range(lanes)]
        )
    down = total_down.astype(bf16)
    whole_row = (jnp.arange(buffer, dtype=i32) // capacity) * rows + place_row
    to_row = (jnp.arange(groups * rows, dtype=i32)[:, None] == whole_row[None, :]).astype(bf16)
    spaced_down = [
        jnp.where(
            mine[:, :, None], down[:, None, t * rank : (t + 1) * rank], jnp.zeros((), bf16)
        ).reshape(buffer, holder_adapters * rank)
        for t in range(2)
    ]
    terms = jnp.stack(
        [jnp.dot(to_row, s, preferred_element_type=f32).astype(bf16) for s in spaced_down]
    )

    order = [reversed_bits(i, bits) for i in range(groups)]
    spread = spread.reshape(groups, rows, -1)
    terms = terms.reshape(2, groups, rows, -1)
    x = jnp.concatenate([lax.dynamic_index_in_dim(spread, group ^ b, 0, False) for b in order], 0)
    d = jnp.concatenate([lax.dynamic_index_in_dim(terms, group ^ b, 1, False) for b in order], 1)

    live = row_index < counts[group]
    chunk_width = extent // CHUNKS
    pieces = []
    for chunk in range(CHUNKS):
        own, other = partial_sums(x, d, gate_up, adapter_up, chunk, chunk_width, chunk_width // 2 if chunk_width % 256 == 0 else chunk_width)
        received = [lax.ppermute(other, "dp", [(i, i ^ 1) for i in range(groups)])]
        extents = groups * rows // 2
        for stage in range(1, bits):
            extents //= 2
            parts = [a[:, extents : 2 * extents].astype(f32) for a in [own] + received]
            message = functools.reduce(jnp.add, parts).astype(bf16)
            received.append(
                lax.ppermute(message, "dp", [(i, i ^ (1 << stage)) for i in range(groups)])
            )
        gate, up = functools.reduce(
            jnp.add, [a[:, :rows].astype(f32) for a in [own] + received]
        )
        hidden = jnp.where(live[:, None], jax.nn.silu(gate) * up, 0.0)
        pieces.append(hidden.astype(bf16))
    return jnp.concatenate(pieces, axis=1)


def solution(mesh):
    placed = (
        P("dp", None),
        P("dp", None, "tensor"),
        P("dp", "tensor", None),
        P("dp", None, None, "tensor"),
        P("dp"),
        P(),
        P(),
    )
    return jax.shard_map(
        body, mesh=mesh, in_specs=placed, out_specs=P("dp", "tensor"), check_vma=False
    )
```

```python
import functools

import jax
import jax.numpy as jnp
from jax import lax
from jax.experimental import pallas as pl
from jax.experimental.pallas import tpu as pltpu
from jax.sharding import PartitionSpec as P

UNITS = 28
WIDTHS = (2, 2, 4, 4, 4, 4, 4, 2, 2)
BLOCK = 256
HOLD = 1
AHEAD = 2
LANE = 128


def interleave_kernel(x_ref, out_ref):
    source = lax.broadcasted_iota(jnp.int32, (LANE, 2 * LANE), 0)
    target = lax.broadcasted_iota(jnp.int32, (LANE, 2 * LANE), 1)
    for t in range(2):
        spacer = (target == 2 * source + t).astype(jnp.bfloat16)
        for j in range(x_ref.shape[1] // LANE):
            spaced = jnp.dot(
                x_ref[:, j * LANE : (j + 1) * LANE], spacer, preferred_element_type=jnp.float32
            )
            out_ref[t, :, 2 * j * LANE : 2 * (j + 1) * LANE] = spaced.astype(jnp.bfloat16)


def interleave(x):
    rows, depth = x.shape
    return pl.pallas_call(
        interleave_kernel,
        out_shape=jax.ShapeDtypeStruct((2, rows, 2 * depth), jnp.bfloat16),
        compiler_params=pltpu.CompilerParams(vmem_limit_bytes=32 * 2**20),
    )(x)


def partial_kernel(x_ref, d_ref, w_ref, u_ref, *rest):
    own_ref, other_ref = rest[-2:]
    half = own_ref.shape[1]
    w = w_ref[...].reshape(2 * w_ref.shape[0], w_ref.shape[2])
    u = u_ref[...].reshape(2 * u_ref.shape[0], u_ref.shape[2])
    for t in range(2):
        total = jnp.dot(x_ref[t], w, preferred_element_type=jnp.float32)
        total = total + jnp.dot(d_ref[t], u, preferred_element_type=jnp.float32)
        own_ref[t] = total[:half]
        other_ref[t] = total[half:].astype(jnp.bfloat16)


def partial_sums(x, d, w, u, end, width, block, after):
    _, rows, depth = x.shape
    inner = d.shape[2]
    first = (end - width) // block
    return pl.pallas_call(
        partial_kernel,
        grid=(width // block,),
        in_specs=[
            pl.BlockSpec((2, rows, depth), lambda j: (0, 0, 0)),
            pl.BlockSpec((2, rows, inner), lambda j: (0, 0, 0)),
            pl.BlockSpec((depth // 2, 2, block), lambda j: (0, 0, first + j)),
            pl.BlockSpec((inner // 2, 2, block), lambda j: (0, 0, first + j)),
        ]
        + [pl.BlockSpec(memory_space=pl.ANY)] * len(after),
        out_specs=[
            pl.BlockSpec((2, rows // 2, block), lambda j: (0, 0, j)),
            pl.BlockSpec((2, rows // 2, block), lambda j: (0, 0, j)),
        ],
        out_shape=[
            jax.ShapeDtypeStruct((2, rows // 2, width), jnp.float32),
            jax.ShapeDtypeStruct((2, rows // 2, width), jnp.bfloat16),
        ],
        compiler_params=pltpu.CompilerParams(vmem_limit_bytes=32 * 2**20),
        cost_estimate=pl.CostEstimate(
            flops=4 * rows * (depth + inner) * width,
            bytes_accessed=2 * (depth + inner) * width + 6 * rows * width,
            transcendentals=0,
        ),
    )(x, d, w, u, *after)


def reversed_bits(value, bits):
    out = 0
    for _ in range(bits):
        out = out * 2 + value % 2
        value //= 2
    return out


def body(
    requests,
    base_gate_up_weight,
    adapter_down_weight,
    adapter_up_weight,
    request_adapter,
    adapter_position,
    counts,
):
    rows, width = requests.shape
    groups = lax.axis_size("dp")
    lanes = lax.axis_size("tensor")
    holder_adapters, depth_part, rank_doubled = adapter_down_weight.shape
    rank = rank_doubled // 2
    extent = adapter_up_weight.shape[3]
    capacity = rows // 8
    buffer = groups * capacity
    group = lax.axis_index("dp")
    lane = lax.axis_index("tensor")
    bits = groups.bit_length() - 1
    f32, bf16, i32 = jnp.float32, jnp.bfloat16, jnp.int32

    match = request_adapter[:, None] == jnp.arange(adapter_position.shape[0], dtype=i32)[None, :]
    slot = jnp.sum(jnp.where(match, adapter_position[None, :], 0), axis=1)
    owner = slot // holder_adapters
    local = slot % holder_adapters
    owner_hot = (owner[:, None] == jnp.arange(groups, dtype=i32)[None, :]).astype(i32)
    place = jnp.sum(owner_hot * (jnp.cumsum(owner_hot, axis=0) - 1), axis=1)
    target = owner * capacity + place
    select = (target[None, :] == jnp.arange(buffer, dtype=i32)[:, None]).astype(bf16)
    row_index = jnp.arange(rows, dtype=i32)
    piece = lax.dynamic_slice_in_dim(requests, lane * depth_part, depth_part, 1)
    column = jnp.arange(LANE, dtype=i32)[None, :]
    labels = jnp.where(column == 0, local[:, None], jnp.where(column == 1, row_index[:, None], 0))
    outgoing = jnp.dot(
        select, jnp.concatenate([piece, labels.astype(bf16)], axis=1), preferred_element_type=f32
    ).astype(bf16)

    part = width // groups
    share = rows // lanes
    extra = capacity * outgoing.shape[1] // part
    mine = lax.dynamic_slice_in_dim(requests, lane * share, share, 0)
    sent = jnp.concatenate(
        [
            mine.reshape(share, groups, part).transpose(1, 0, 2),
            outgoing.reshape(groups, extra, part),
        ],
        axis=1,
    )
    came = lax.all_to_all(sent, "dp", split_axis=0, concat_axis=0, tiled=True)
    spread = came[:, :share]
    arrived = came[:, share:].reshape(buffer, outgoing.shape[1])

    def over_lanes(array, mask):
        return lax.ppermute(array, "tensor", [(i, i ^ mask) for i in range(lanes)])

    spread = jnp.stack([spread] + [over_lanes(spread, k) for k in range(1, lanes)])

    which = arrived[:, depth_part].astype(i32)
    place_row = arrived[:, depth_part + 1].astype(i32)
    mine = which[:, None] == jnp.arange(holder_adapters, dtype=i32)[None, :]
    routed = arrived[:, :depth_part]
    spaced = jnp.where(mine[:, :, None], routed[:, None, :], jnp.zeros((), bf16))
    part_down = jnp.dot(
        spaced.reshape(buffer, holder_adapters * depth_part),
        adapter_down_weight.reshape(holder_adapters * depth_part, rank_doubled),
        preferred_element_type=f32,
    )
    total_down = part_down
    for k in range(1, lanes):
        total_down = total_down + over_lanes(part_down, k)
    down = total_down.astype(bf16)
    whole_row = (jnp.arange(buffer, dtype=i32) // capacity) * rows + place_row
    to_row = (jnp.arange(groups * rows, dtype=i32)[:, None] == whole_row[None, :]).astype(bf16)
    terms = []
    for t in range(2):
        spacer = 2 * jnp.arange(rank, dtype=i32)[:, None] + t == jnp.arange(2 * rank)[None, :]
        apart = jnp.dot(
            down[:, t * rank : (t + 1) * rank], spacer.astype(bf16), preferred_element_type=f32
        ).astype(bf16)
        apart = jnp.where(mine[:, :, None], apart[:, None, :], jnp.zeros((), bf16))
        apart = apart.reshape(buffer, holder_adapters * 2 * rank)
        terms.append(jnp.dot(to_row, apart, preferred_element_type=f32).astype(bf16))
    terms = jnp.stack(terms).reshape(2, groups, rows, -1)

    order = [reversed_bits(i, bits) for i in range(groups)]
    x = jnp.concatenate(
        [
            lax.dynamic_slice(spread, (lane ^ k, group ^ b, 0, 0), (1, 1, share, part))[0, 0]
            for b in order
            for k in range(lanes)
        ],
        0,
    )
    x = interleave(x)
    d = jnp.concatenate([lax.dynamic_index_in_dim(terms, group ^ b, 1, False) for b in order], 1)
    adapter_up = adapter_up_weight.reshape(holder_adapters * rank, 2, extent)

    live = row_index < counts[group]
    unit = extent // UNITS
    ends = [unit * sum(WIDTHS[: i + 1]) for i in range(len(WIDTHS))]
    count = len(WIDTHS)
    stages = [[] for _ in WIDTHS]
    pieces = []

    def send(array, mask):
        return lax.ppermute(array, "dp", [(i, i ^ mask) for i in range(groups)])

    def begin(chunk, after):
        own, other = partial_sums(
            x, d, base_gate_up_weight, adapter_up, ends[chunk], unit * WIDTHS[chunk], BLOCK, after
        )
        stages[chunk] = [own, send(other, 1)]

    def advance(chunk, stage):
        size = groups * rows >> (stage + 1)
        parts = [a[:, size : 2 * size].astype(f32) for a in stages[chunk]]
        message = functools.reduce(jnp.add, parts).astype(bf16)
        stages[chunk].append(send(message, 1 << stage))
        return message

    def finish(chunk, after):
        if HOLD:
            stages[chunk], after = lax.optimization_barrier((stages[chunk], after))
        gate, up = functools.reduce(jnp.add, [a[:, :rows].astype(f32) for a in stages[chunk]])
        hidden = jnp.where(live[:, None], jax.nn.silu(gate) * up, 0.0)
        pieces.append(hidden.astype(bf16))

    for chunk in range(min(AHEAD, count)):
        begin(chunk, [])
    for slot in range(count + bits - 1):
        after = [
            advance(slot - stage + 1, stage)
            for stage in range(1, bits)
            if 0 <= slot - stage + 1 < count
        ]
        if slot + AHEAD < count:
            begin(slot + AHEAD, after)
        if 0 <= slot - bits + 1 < count:
            finish(slot - bits + 1, after)
    return jnp.concatenate(pieces, axis=1)


def solution(mesh):
    placed = (
        P("dp", None),
        P("dp", None, "tensor"),
        P("dp", "tensor", None),
        P("dp", None, None, "tensor"),
        P("dp"),
        P(),
        P(),
    )
    return jax.shard_map(
        body, mesh=mesh, in_specs=placed, out_specs=P("dp", "tensor"), check_vma=False
    )
```

```python
import functools

import jax
import jax.numpy as jnp
from jax import lax
from jax.experimental import pallas as pl
from jax.experimental.pallas import tpu as pltpu
from jax.sharding import PartitionSpec as P

UNITS = 28
WIDTHS = (2, 4, 5, 5, 5, 4, 3)
AHEAD = 2
BATCHES = ()
HOLD = 1
CHAIN = 1
LANE = 128


def interleave_kernel(x_ref, out_ref):
    source = lax.broadcasted_iota(jnp.int32, (LANE, 2 * LANE), 0)
    target = lax.broadcasted_iota(jnp.int32, (LANE, 2 * LANE), 1)
    for t in range(2):
        spacer = (target == 2 * source + t).astype(jnp.bfloat16)
        for j in range(x_ref.shape[1] // LANE):
            spaced = jnp.dot(
                x_ref[:, j * LANE : (j + 1) * LANE], spacer, preferred_element_type=jnp.float32
            )
            out_ref[t, :, 2 * j * LANE : 2 * (j + 1) * LANE] = spaced.astype(jnp.bfloat16)


def interleave(x):
    rows, depth = x.shape
    return pl.pallas_call(
        interleave_kernel,
        out_shape=jax.ShapeDtypeStruct((2, rows, 2 * depth), jnp.bfloat16),
        compiler_params=pltpu.CompilerParams(vmem_limit_bytes=32 * 2**20),
    )(x)


def partial_kernel(x_ref, d_ref, w_ref, u_ref, *rest):
    own_ref, other_ref = rest[-2:]
    half = own_ref.shape[1]
    w = w_ref[...].reshape(2 * w_ref.shape[0], w_ref.shape[2])
    u = u_ref[...].reshape(2 * u_ref.shape[0], u_ref.shape[2])
    for t in range(2):
        total = jnp.dot(x_ref[t], w, preferred_element_type=jnp.float32)
        total = total + jnp.dot(d_ref[t], u, preferred_element_type=jnp.float32)
        own_ref[t] = total[:half]
        other_ref[t] = total[half:].astype(jnp.bfloat16)


def partial_sums(x, d, w, u, end, width, block, after):
    _, rows, depth = x.shape
    inner = d.shape[2]
    first = (end - width) // block
    return pl.pallas_call(
        partial_kernel,
        grid=(width // block,),
        in_specs=[
            pl.BlockSpec((2, rows, depth), lambda j: (0, 0, 0)),
            pl.BlockSpec((2, rows, inner), lambda j: (0, 0, 0)),
            pl.BlockSpec((depth // 2, 2, block), lambda j: (0, 0, first + j)),
            pl.BlockSpec((inner // 2, 2, block), lambda j: (0, 0, first + j)),
        ]
        + [pl.BlockSpec(memory_space=pl.ANY)] * len(after),
        out_specs=[
            pl.BlockSpec((2, rows // 2, block), lambda j: (0, 0, j)),
            pl.BlockSpec((2, rows // 2, block), lambda j: (0, 0, j)),
        ],
        out_shape=[
            jax.ShapeDtypeStruct((2, rows // 2, width), jnp.float32),
            jax.ShapeDtypeStruct((2, rows // 2, width), jnp.bfloat16),
        ],
        compiler_params=pltpu.CompilerParams(vmem_limit_bytes=42 * 2**20),
        cost_estimate=pl.CostEstimate(
            flops=4 * rows * (depth + inner) * width,
            bytes_accessed=2 * (depth + inner) * width + 6 * rows * width,
            transcendentals=0,
        ),
    )(x, d, w, u, *after)


def reversed_bits(value, bits):
    out = 0
    for _ in range(bits):
        out = out * 2 + value % 2
        value //= 2
    return out


def body(
    requests,
    base_gate_up_weight,
    adapter_down_weight,
    adapter_up_weight,
    request_adapter,
    adapter_position,
    counts,
):
    rows, width = requests.shape
    groups = lax.axis_size("dp")
    lanes = lax.axis_size("tensor")
    holder_adapters, depth_part, rank_doubled = adapter_down_weight.shape
    rank = rank_doubled // 2
    extent = adapter_up_weight.shape[3]
    capacity = rows // 8
    buffer = groups * capacity
    group = lax.axis_index("dp")
    lane = lax.axis_index("tensor")
    bits = groups.bit_length() - 1
    f32, bf16, i32 = jnp.float32, jnp.bfloat16, jnp.int32

    match = request_adapter[:, None] == jnp.arange(adapter_position.shape[0], dtype=i32)[None, :]
    slot = jnp.sum(jnp.where(match, adapter_position[None, :], 0), axis=1)
    owner = slot // holder_adapters
    local = slot % holder_adapters
    owner_hot = (owner[:, None] == jnp.arange(groups, dtype=i32)[None, :]).astype(i32)
    place = jnp.sum(owner_hot * (jnp.cumsum(owner_hot, axis=0) - 1), axis=1)
    target = owner * capacity + place
    select = (target[None, :] == jnp.arange(buffer, dtype=i32)[:, None]).astype(bf16)
    row_index = jnp.arange(rows, dtype=i32)
    piece = lax.dynamic_slice_in_dim(requests, lane * depth_part, depth_part, 1)
    column = jnp.arange(LANE, dtype=i32)[None, :]
    labels = jnp.where(column == 0, local[:, None], jnp.where(column == 1, row_index[:, None], 0))
    outgoing = jnp.dot(
        select, jnp.concatenate([piece, labels.astype(bf16)], axis=1), preferred_element_type=f32
    ).astype(bf16)

    part = width // groups
    share = rows // lanes
    extra = capacity * outgoing.shape[1] // part
    mine = lax.dynamic_slice_in_dim(requests, lane * share, share, 0)
    sent = jnp.concatenate(
        [
            mine.reshape(share, groups, part).transpose(1, 0, 2),
            outgoing.reshape(groups, extra, part),
        ],
        axis=1,
    )
    came = lax.all_to_all(sent, "dp", split_axis=0, concat_axis=0, tiled=True)
    spread = came[:, :share]
    arrived = came[:, share:].reshape(buffer, outgoing.shape[1])

    def over_lanes(array, mask):
        return lax.ppermute(array, "tensor", [(i, i ^ mask) for i in range(lanes)])

    spread = jnp.concatenate([spread] + [over_lanes(spread, k) for k in range(1, lanes)], 0)
    spread = spread.reshape(groups * rows, part)

    which = arrived[:, depth_part].astype(i32)
    place_row = arrived[:, depth_part + 1].astype(i32)
    mine = which[:, None] == jnp.arange(holder_adapters, dtype=i32)[None, :]
    routed = arrived[:, :depth_part]
    spaced = jnp.where(mine[:, :, None], routed[:, None, :], jnp.zeros((), bf16))
    part_down = jnp.dot(
        spaced.reshape(buffer, holder_adapters * depth_part),
        adapter_down_weight.reshape(holder_adapters * depth_part, rank_doubled),
        preferred_element_type=f32,
    )
    total_down = part_down
    for k in range(1, lanes):
        total_down = total_down + over_lanes(part_down, k)
    down = total_down.astype(bf16)
    order = jnp.array([reversed_bits(i, bits) for i in range(groups)], i32)
    pack = 3 * rows // 4
    before = jnp.cumsum(counts) - counts

    def position(of_group, of_row):
        near = of_group[:, None] == jnp.arange(groups, dtype=i32)[None, :]
        start = jnp.sum(jnp.where(near, before[None, :], 0), axis=1)
        limit = jnp.sum(jnp.where(near, counts[None, :], 0), axis=1)
        return jnp.where(of_row < limit, start + of_row, -groups * rows)

    number = jnp.arange(groups * rows, dtype=i32)
    from_lane = lane ^ (number // (groups * share))
    came_at = position(number // share % groups, from_lane * share + number % share)
    packed = ((group ^ order)[:, None] * pack + jnp.arange(pack, dtype=i32)[None, :]).reshape(-1)
    pick = (packed[:, None] == came_at[None, :]).astype(bf16)
    slot_at = position(jnp.arange(buffer, dtype=i32) // capacity, place_row)
    to_row = (packed[:, None] == slot_at[None, :]).astype(bf16)
    terms = []
    for t in range(2):
        spacer = 2 * jnp.arange(rank, dtype=i32)[:, None] + t == jnp.arange(2 * rank)[None, :]
        apart = jnp.dot(
            down[:, t * rank : (t + 1) * rank], spacer.astype(bf16), preferred_element_type=f32
        ).astype(bf16)
        apart = jnp.where(mine[:, :, None], apart[:, None, :], jnp.zeros((), bf16))
        apart = apart.reshape(buffer, holder_adapters * 2 * rank)
        terms.append(jnp.dot(to_row, apart, preferred_element_type=f32).astype(bf16))
    d = jnp.stack(terms)
    x = interleave(jnp.dot(pick, spread, preferred_element_type=f32).astype(bf16))
    adapter_up = adapter_up_weight.reshape(holder_adapters * rank, 2, extent)

    chips = groups // 2
    total = groups * pack
    reach = 0
    for chip in range(chips):
        low = max(0, total - 2 * rows * (chips - chip)) // (2 * pack)
        high = (min(2 * rows * (chip + 1), total) - 1) // (2 * pack)
        reach = max(reach, chip - low, high - chip)
    shifts = [0] + [k * sign for k in range(1, reach + 1) for sign in (1, -1)]
    both = jnp.concatenate([jnp.full((rows,), group), jnp.full((rows,), group ^ 1)])
    wanted = position(both, jnp.concatenate([row_index, row_index]))
    held = jnp.concatenate(
        [(group + 2 * k) * pack + jnp.arange(pack, dtype=i32) for k in shifts]
    )
    give = (wanted[:, None] == held[None, :]).astype(bf16)

    unit = extent // UNITS
    ends = [unit * sum(WIDTHS[: i + 1]) for i in range(len(WIDTHS))]
    count = len(WIDTHS)
    stages = [[] for _ in WIDTHS]
    pieces = []

    def send(array, mask):
        return lax.ppermute(array, "dp", [(i, i ^ mask) for i in range(groups)])

    def begin(chunk, after):
        own, other = partial_sums(
            x, d, base_gate_up_weight, adapter_up, ends[chunk], unit * WIDTHS[chunk], unit, after
        )
        stages[chunk] = [own, send(other, 1)]

    def advance(chunk, stage):
        size = total >> (stage + 1)
        if CHAIN and stage in last:
            stages[chunk], _ = lax.optimization_barrier((stages[chunk], last[stage]))
        parts = [a[:, size : 2 * size].astype(f32) for a in stages[chunk]]
        message = functools.reduce(jnp.add, parts).astype(bf16)
        stages[chunk].append(send(message, 1 << stage))
        if stage > 1:
            last[stage] = message
        return message

    def finish(chunk, after):
        if HOLD:
            stages[chunk], after = lax.optimization_barrier((stages[chunk], after))
        gate, up = functools.reduce(jnp.add, [a[:, :pack].astype(f32) for a in stages[chunk]])
        pieces.append((jax.nn.silu(gate) * up).astype(bf16))

    def deliver():
        mine = jnp.concatenate(pieces, axis=1)
        pieces.clear()
        near = [mine] + [
            lax.ppermute(
                mine,
                "dp",
                [(i + 2 * k, i) for i in range(groups) if 0 <= i + 2 * k < groups],
            )
            for k in shifts[1:]
        ]
        chosen = jnp.dot(give, jnp.concatenate(near, 0), preferred_element_type=f32).astype(bf16)
        outputs.append(chosen[:rows] + send(chosen[rows:], 1))
        return chosen

    outputs = []
    last = {}
    for chunk in range(min(AHEAD, count)):
        begin(chunk, [])
    for slot in range(count + bits - 1):
        after = [
            advance(slot - stage + 1, stage)
            for stage in range(1, bits)
            if 0 <= slot - stage + 1 < count
        ]
        done = slot - bits + 1
        if done - 1 in BATCHES:
            after.append(deliver())
        if slot + AHEAD < count:
            begin(slot + AHEAD, after)
        if 0 <= done < count:
            finish(done, after)
    deliver()
    return jnp.concatenate(outputs, axis=1)


def solution(mesh):
    placed = (
        P("dp", None),
        P("dp", None, "tensor"),
        P("dp", "tensor", None),
        P("dp", None, None, "tensor"),
        P("dp"),
        P(),
        P(),
    )
    return jax.shard_map(
        body, mesh=mesh, in_specs=placed, out_specs=P("dp", "tensor"), check_vma=False
    )
```

```python
import functools

import jax
import jax.numpy as jnp
from jax import lax
from jax.experimental import pallas as pl
from jax.experimental.pallas import tpu as pltpu
from jax.sharding import PartitionSpec as P

UNITS = 28
WIDTHS = (1, 3, 5, 5, 6, 5, 3)
AHEAD = 2
BATCHES = ()
HOLD = 1
CHAIN = 1
LANE = 128


def interleave_kernel(x_ref, out_ref):
    source = lax.broadcasted_iota(jnp.int32, (LANE, 2 * LANE), 0)
    target = lax.broadcasted_iota(jnp.int32, (LANE, 2 * LANE), 1)
    for t in range(2):
        spacer = (target == 2 * source + t).astype(jnp.bfloat16)
        for j in range(x_ref.shape[1] // LANE):
            spaced = jnp.dot(
                x_ref[:, j * LANE : (j + 1) * LANE], spacer, preferred_element_type=jnp.float32
            )
            out_ref[t, :, 2 * j * LANE : 2 * (j + 1) * LANE] = spaced.astype(jnp.bfloat16)


def interleave(x):
    rows, depth = x.shape
    return pl.pallas_call(
        interleave_kernel,
        out_shape=jax.ShapeDtypeStruct((2, rows, 2 * depth), jnp.bfloat16),
        compiler_params=pltpu.CompilerParams(vmem_limit_bytes=32 * 2**20),
    )(x)


def partial_kernel(x_ref, d_ref, w_ref, u_ref, *rest):
    own_ref, other_ref = rest[-2:]
    half = own_ref.shape[1]
    w = w_ref[...].reshape(2 * w_ref.shape[0], w_ref.shape[2])
    u = u_ref[...].reshape(2 * u_ref.shape[0], u_ref.shape[2])
    for t in range(2):
        total = jnp.dot(x_ref[t], w, preferred_element_type=jnp.float32)
        total = total + jnp.dot(d_ref[t], u, preferred_element_type=jnp.float32)
        own_ref[t] = total[:half]
        other_ref[t] = total[half:].astype(jnp.bfloat16)


def partial_sums(x, d, w, u, end, width, block, after):
    _, rows, depth = x.shape
    inner = d.shape[2]
    first = (end - width) // block
    return pl.pallas_call(
        partial_kernel,
        grid=(width // block,),
        in_specs=[
            pl.BlockSpec((2, rows, depth), lambda j: (0, 0, 0)),
            pl.BlockSpec((2, rows, inner), lambda j: (0, 0, 0)),
            pl.BlockSpec((depth // 2, 2, block), lambda j: (0, 0, first + j)),
            pl.BlockSpec((inner // 2, 2, block), lambda j: (0, 0, first + j)),
        ]
        + [pl.BlockSpec(memory_space=pl.ANY)] * len(after),
        out_specs=[
            pl.BlockSpec((2, rows // 2, block), lambda j: (0, 0, j)),
            pl.BlockSpec((2, rows // 2, block), lambda j: (0, 0, j)),
        ],
        out_shape=[
            jax.ShapeDtypeStruct((2, rows // 2, width), jnp.float32),
            jax.ShapeDtypeStruct((2, rows // 2, width), jnp.bfloat16),
        ],
        compiler_params=pltpu.CompilerParams(vmem_limit_bytes=42 * 2**20),
        cost_estimate=pl.CostEstimate(
            flops=4 * rows * (depth + inner) * width,
            bytes_accessed=2 * (depth + inner) * width + 6 * rows * width,
            transcendentals=0,
        ),
    )(x, d, w, u, *after)


def reversed_bits(value, bits):
    out = 0
    for _ in range(bits):
        out = out * 2 + value % 2
        value //= 2
    return out


def body(
    requests,
    base_gate_up_weight,
    adapter_down_weight,
    adapter_up_weight,
    request_adapter,
    adapter_position,
    counts,
):
    rows, width = requests.shape
    groups = lax.axis_size("dp")
    lanes = lax.axis_size("tensor")
    holder_adapters, depth_part, rank_doubled = adapter_down_weight.shape
    rank = rank_doubled // 2
    extent = adapter_up_weight.shape[3]
    capacity = rows // 8
    buffer = groups * capacity
    group = lax.axis_index("dp")
    lane = lax.axis_index("tensor")
    bits = groups.bit_length() - 1
    f32, bf16, i32 = jnp.float32, jnp.bfloat16, jnp.int32

    match = request_adapter[:, None] == jnp.arange(adapter_position.shape[0], dtype=i32)[None, :]
    slot = jnp.sum(jnp.where(match, adapter_position[None, :], 0), axis=1)
    owner = slot // holder_adapters
    local = slot % holder_adapters
    owner_hot = (owner[:, None] == jnp.arange(groups, dtype=i32)[None, :]).astype(i32)
    place = jnp.sum(owner_hot * (jnp.cumsum(owner_hot, axis=0) - 1), axis=1)
    target = owner * capacity + place
    select = (target[None, :] == jnp.arange(buffer, dtype=i32)[:, None]).astype(bf16)
    row_index = jnp.arange(rows, dtype=i32)
    piece = lax.dynamic_slice_in_dim(requests, lane * depth_part, depth_part, 1)
    column = jnp.arange(LANE, dtype=i32)[None, :]
    labels = jnp.where(column == 0, local[:, None], jnp.where(column == 1, row_index[:, None], 0))
    outgoing = jnp.dot(
        select, jnp.concatenate([piece, labels.astype(bf16)], axis=1), preferred_element_type=f32
    ).astype(bf16)

    part = width // groups
    share = rows // lanes
    extra = capacity * outgoing.shape[1] // part
    mine = lax.dynamic_slice_in_dim(requests, lane * share, share, 0)
    sent = jnp.concatenate(
        [
            mine.reshape(share, groups, part).transpose(1, 0, 2),
            outgoing.reshape(groups, extra, part),
        ],
        axis=1,
    )
    came = lax.all_to_all(sent, "dp", split_axis=0, concat_axis=0, tiled=True)
    spread = came[:, :share]
    arrived = came[:, share:].reshape(buffer, outgoing.shape[1])

    def over_lanes(array, mask):
        return lax.ppermute(array, "tensor", [(i, i ^ mask) for i in range(lanes)])

    spread = jnp.concatenate([spread] + [over_lanes(spread, k) for k in range(1, lanes)], 0)
    spread = spread.reshape(groups * rows, part)

    which = arrived[:, depth_part].astype(i32)
    place_row = arrived[:, depth_part + 1].astype(i32)
    mine = which[:, None] == jnp.arange(holder_adapters, dtype=i32)[None, :]
    routed = arrived[:, :depth_part]
    spaced = jnp.where(mine[:, :, None], routed[:, None, :], jnp.zeros((), bf16))
    part_down = jnp.dot(
        spaced.reshape(buffer, holder_adapters * depth_part),
        adapter_down_weight.reshape(holder_adapters * depth_part, rank_doubled),
        preferred_element_type=f32,
    )
    total_down = part_down
    for k in range(1, lanes):
        total_down = total_down + over_lanes(part_down, k)
    down = total_down.astype(bf16)
    order = jnp.array([reversed_bits(i, bits) for i in range(groups)], i32)
    pack = 3 * rows // 4
    before = jnp.cumsum(counts) - counts

    def position(of_group, of_row):
        near = of_group[:, None] == jnp.arange(groups, dtype=i32)[None, :]
        start = jnp.sum(jnp.where(near, before[None, :], 0), axis=1)
        limit = jnp.sum(jnp.where(near, counts[None, :], 0), axis=1)
        return jnp.where(of_row < limit, start + of_row, -groups * rows)

    number = jnp.arange(groups * rows, dtype=i32)
    from_lane = lane ^ (number // (groups * share))
    came_at = position(number // share % groups, from_lane * share + number % share)
    packed = ((group ^ order)[:, None] * pack + jnp.arange(pack, dtype=i32)[None, :]).reshape(-1)
    pick = (packed[:, None] == came_at[None, :]).astype(bf16)
    slot_at = position(jnp.arange(buffer, dtype=i32) // capacity, place_row)
    to_row = (packed[:, None] == slot_at[None, :]).astype(bf16)
    terms = []
    for t in range(2):
        spacer = 2 * jnp.arange(rank, dtype=i32)[:, None] + t == jnp.arange(2 * rank)[None, :]
        apart = jnp.dot(
            down[:, t * rank : (t + 1) * rank], spacer.astype(bf16), preferred_element_type=f32
        ).astype(bf16)
        apart = jnp.where(mine[:, :, None], apart[:, None, :], jnp.zeros((), bf16))
        apart = apart.reshape(buffer, holder_adapters * 2 * rank)
        terms.append(jnp.dot(to_row, apart, preferred_element_type=f32).astype(bf16))
    d = jnp.stack(terms)
    x = interleave(jnp.dot(pick, spread, preferred_element_type=f32).astype(bf16))
    adapter_up = adapter_up_weight.reshape(holder_adapters * rank, 2, extent)

    chips = groups // 2
    total = groups * pack
    reach = 0
    for chip in range(chips):
        low = max(0, total - 2 * rows * (chips - chip)) // (2 * pack)
        high = (min(2 * rows * (chip + 1), total) - 1) // (2 * pack)
        reach = max(reach, chip - low, high - chip)
    shifts = [0] + [k * sign for k in range(1, reach + 1) for sign in (1, -1)]
    both = jnp.concatenate([jnp.full((rows,), group), jnp.full((rows,), group ^ 1)])
    wanted = position(both, jnp.concatenate([row_index, row_index]))
    held = jnp.concatenate(
        [(group + 2 * k) * pack + jnp.arange(pack, dtype=i32) for k in shifts]
    )
    give = (wanted[:, None] == held[None, :]).astype(bf16)

    unit = extent // UNITS
    ends = [unit * sum(WIDTHS[: i + 1]) for i in range(len(WIDTHS))]
    count = len(WIDTHS)
    stages = [[] for _ in WIDTHS]
    pieces = []

    def send(array, mask):
        return lax.ppermute(array, "dp", [(i, i ^ mask) for i in range(groups)])

    def begin(chunk, after):
        own, other = partial_sums(
            x, d, base_gate_up_weight, adapter_up, ends[chunk], unit * WIDTHS[chunk], unit, after
        )
        stages[chunk] = [own, send(other, 1)]

    def advance(chunk, stage):
        size = total >> (stage + 1)
        if CHAIN and stage in last:
            stages[chunk], _ = lax.optimization_barrier((stages[chunk], last[stage]))
        parts = [a[:, size : 2 * size].astype(f32) for a in stages[chunk]]
        message = functools.reduce(jnp.add, parts).astype(bf16)
        stages[chunk].append(send(message, 1 << stage))
        if stage > 1:
            last[stage] = message
        return message

    def finish(chunk, after):
        if HOLD:
            stages[chunk], after = lax.optimization_barrier((stages[chunk], after))
        gate, up = functools.reduce(jnp.add, [a[:, :pack].astype(f32) for a in stages[chunk]])
        pieces.append((jax.nn.silu(gate) * up).astype(bf16))

    def deliver():
        mine = jnp.concatenate(pieces, axis=1)
        pieces.clear()
        near = [mine] + [
            lax.ppermute(
                mine,
                "dp",
                [(i + 2 * k, i) for i in range(groups) if 0 <= i + 2 * k < groups],
            )
            for k in shifts[1:]
        ]
        chosen = jnp.dot(give, jnp.concatenate(near, 0), preferred_element_type=f32).astype(bf16)
        outputs.append(chosen[:rows] + send(chosen[rows:], 1))
        return chosen

    outputs = []
    last = {}
    for chunk in range(min(AHEAD, count)):
        begin(chunk, [])
    for slot in range(count + bits - 1):
        after = [
            advance(slot - stage + 1, stage)
            for stage in range(1, bits)
            if 0 <= slot - stage + 1 < count
        ]
        done = slot - bits + 1
        if done - 1 in BATCHES:
            after.append(deliver())
        if slot + AHEAD < count:
            begin(slot + AHEAD, after)
        if 0 <= done < count:
            finish(done, after)
    deliver()
    return jnp.concatenate(outputs, axis=1)


def solution(mesh):
    placed = (
        P("dp", None),
        P("dp", None, "tensor"),
        P("dp", "tensor", None),
        P("dp", None, None, "tensor"),
        P("dp"),
        P(),
        P(),
    )
    return jax.shard_map(
        body, mesh=mesh, in_specs=placed, out_specs=P("dp", "tensor"), check_vma=False
    )
```
